256 devices in a mesh: aux: 4 (over x), blk: 32 (over z, y), occ: 2 (over core).
Axes of the slice: x: 4, y: 4, z: 8, core: 2. Of those that a mesh axis runs over, the one named last changes fastest.
Arguments:
- integrals: bfloat16 [16, 32, 11, 512, 512], P('aux', 'blk'), may hold values from -0.078125 to 0.078125
- orbitals: bfloat16 [16384, 512], P('blk', 'occ'), may hold values from -6 to 6
- pair_lists: int32 [32, 11], P('blk'), may hold values from 0 to 31, as said below
- pair_counts: int32 [32], P('blk'), may hold values from 1 to 11, as said below
Outputs:
- exchange: float32 [32, 512, 512], P('blk', 'aux')
The draws below stay inside these ranges and needn't reach their ends.
Inputs may be any that keep to these rules, and one draw needn't show every extreme that they name: `pair_lists`: entry 0 of row m is m itself; entries past pair_counts[m] are never read. `pair_counts`: some block has all 11 slots live.
All inputs are finite; a program needn't handle non-finite values.
Results may differ from the reference program's by a relative error of at most 0.00099.
Values may be sent and summed in bfloat16 or wider, within the bound.
A program may use at most 192 MiB of HBM per device.

```python
import jax
import jax.numpy as jnp
from jax import lax

BS = 512
SLOTS = 11
NOCC = 512
NB = 32
NBAS = 16384
NAUX = 16


def fullest_block(key):
    return jax.random.randint(jax.random.fold_in(key, 29), (), 0, NB)


def draw_pair_lists(key, part):
    values = jax.random.randint(jax.random.fold_in(key, 11), (NB, SLOTS), 0, NB)
    rows = jnp.arange(NB, dtype=jnp.int32)
    far_block = (rows + NB // 2) % NB
    choose_far = jax.random.randint(jax.random.fold_in(key, 37), (NB,), 0, 2) == 1
    choose_far = choose_far | (rows == fullest_block(key))
    values = values.at[:, 1].set(jnp.where(choose_far, far_block, values[:, 1]))
    return values.at[:, 0].set(rows).astype(jnp.int32)


def draw_pair_counts(key, part):
    counts = jax.random.randint(jax.random.fold_in(key, 23), (NB,), 1, SLOTS + 1)
    return counts.at[fullest_block(key)].set(SLOTS).astype(jnp.int32)


def steps_of(own_key, extent, split, low, high):
    factor_of = 1.0
    for position, blocks in split:
        steps = jax.random.uniform(jax.random.fold_in(jax.random.fold_in(own_key, 6), position), (blocks,), jnp.float32, low / len(split), high / len(split))
        factor_of = factor_of * jnp.repeat(jnp.exp(steps), extent[position] // blocks).reshape((-1,) + (1,) * (len(extent) - 1 - position))
    return factor_of


def normal_values(key, shape, spread, bound, split=(), held_as=jnp.bfloat16):
    result = jax.random.normal(key, shape, jnp.float32) * spread
    if len(split) > 0:
        result = steps_of(key, shape, split, -0.22, 0.18) * result
    return jnp.clip(result, min=-bound, max=bound).astype(held_as)


def setup_inputs(seed: int = 0) -> dict:
    splits = jax.random.split(jax.random.key(seed), 5)
    return {
        "integrals": normal_values(splits[0], (NAUX, NB, SLOTS, BS, BS), (BS * SLOTS) ** -0.5, 0.078125, ((0, 4), (1, 32))),
        "orbitals": normal_values(splits[1], (NBAS, NOCC), 1.0, 6.0, ((0, 32), (1, 2))),
        "pair_lists": draw_pair_lists(jax.random.fold_in(splits[4], 71), 0),
        "pair_counts": draw_pair_counts(jax.random.fold_in(splits[4], 71), 0),
    }


def reference(integrals, orbitals, pair_lists, pair_counts):
    coef_blocks = orbitals.reshape(NB, BS, NOCC)

    def one_block(block_index):
        block_ints = lax.dynamic_index_in_dim(integrals, block_index, 1, keepdims=False)
        lists = lax.dynamic_index_in_dim(pair_lists, block_index, 0, keepdims=False)
        live = lax.dynamic_index_in_dim(pair_counts, block_index, 0, keepdims=False)
        picked = coef_blocks[lists.astype(jnp.int32)]
        keep = (jnp.arange(SLOTS, dtype=jnp.int32) < live).astype(jnp.float32)
        picked = picked.astype(jnp.float32) * keep[:, None, None]
        half = jnp.einsum("psab,sbi->pai", block_ints.astype(jnp.float32), picked)
        half = half.astype(jnp.bfloat16).astype(jnp.float32)
        return jnp.einsum("pai,pbi->ab", half, half) / NOCC

    return lax.map(one_block, jnp.arange(NB, dtype=jnp.int32))
```

```python
import functools

import jax
import jax.numpy as jnp
from jax import lax
from jax.experimental import pallas as pl
from jax.experimental.pallas import tpu as pltpu
from jax.sharding import PartitionSpec as P

MESH = pl.DeviceIdType.MESH
NX, NY, NZ = 4, 4, 8
BF16, F32 = jnp.bfloat16, jnp.float32

CHUNKS = (
    (0, 128, 4, "quick"),
    (128, 128, 4, "zy"),
    (256, 128, 4, "zy"),
    (384, 128, 4, "zy"),
)


def z_tree(kind):
    if kind == "quick":
        return [(1, 0), (-1, 0), (2, 0), (-2, 0), (3, 2), (-3, -2), (4, 2)]
    return [(1, 0), (-1, 0), (2, 1), (-2, -1), (3, 2), (-3, -2), (4, 3)]


def plane_tree(kind):
    edges = []
    if kind in ("quick", "zy"):
        for node, parent in [(0, None)] + z_tree(kind):
            if parent is not None:
                edges.append(((0, node), (0, parent)))
            for dy in (1, -1, 2):
                edges.append(((dy, node), (0, node)))
    else:
        for dy in (0, 1, -1, 2):
            if dy:
                edges.append(((dy, 0), (0, 0)))
            for node, parent in z_tree("fwd"):
                edges.append(((dy, node), (dy, parent)))
    return edges


def hops(node, parent):
    dy, dz = (node[0] - parent[0]) % NY, (node[1] - parent[1]) % NZ
    return min(dy, NY - dy) + min(dz, NZ - dz)


def schedule(chunks):
    events = []
    x_free = 0.0
    for c, (row, rows, share, kind) in enumerate(chunks):
        edges = plane_tree(kind)
        start = 2.0 * c
        when = {(0, 0): start}
        kids = {}
        for node, parent in edges:
            when[node] = when[parent] + 1.6 + 0.65 * hops(node, parent)
            kids.setdefault(parent, []).append(node)
        for parent, nodes in kids.items():
            events.append((when[parent], "node", c, parent, tuple(nodes)))
        done = max(when.values()) + 1.5
        x_free = max(done, x_free)
        events.append((done, "select", c))
        unit = 15.0 * rows / 512
        if share == 4:
            events.append((x_free + 2.0 + unit / 3, "forward", c))
            x_free += unit
            ready = x_free + 4.0
        elif share == 2:
            x_free += unit / 3
            ready = x_free + 2.0
        else:
            ready = done + 0.5
        for p in range(4):
            events.append((ready + 0.2 * p, "compute", c, p))
    events.sort(key=lambda e: e[0])
    return events


def kernel(
    chunks, ints_hbm, orb_hbm, lists, counts, out_ref,
    ints, orb, acc, half, part, theirs, mine, arrived, other, *refs,
):
    count = len(chunks)
    tables, lands = refs[:count], refs[count : 2 * count]
    (
        int_sem, orb_sem, root_recv, leaf_recv, plane_send, x_recv, x_send,
        core_send, core_recv, sum_send, sum_recv, last_send, last_recv,
    ) = refs[2 * count :]
    slots = ints.shape[1]
    picks = slots - 1
    x = lax.axis_index("aux")
    plane = lax.axis_index("blk")
    core = lax.axis_index("occ")
    y, z = lax.rem(plane, NY), plane // NY

    def device(dx=0, dy=0, dz=0, dc=0):
        return (
            lax.rem(x + (dx + NX), NX),
            lax.rem(z + (dz + NZ), NZ) * NY + lax.rem(y + (dy + NY), NY),
            lax.rem(core + dc, 2),
        )

    def source(dy, dz):
        return lax.rem(z + (NZ - dz), NZ) * NY + lax.rem(y + (NY - dy), NY)

    int_copies = [
        pltpu.make_async_copy(ints_hbm.at[:, 0, s], ints.at[:, s], int_sem.at[s])
        for s in range(slots)
    ]
    orb_copy = pltpu.make_async_copy(orb_hbm, orb, orb_sem)
    orb_copy.start()
    int_copies[0].start()

    partners = {(1, 0, 0, 0), (3, 0, 0, 0), (2, 0, 0, 0), (0, 0, 0, 1)}
    for _, _, _, kind in chunks:
        for node, parent in plane_tree(kind):
            dy, dz = (node[0] - parent[0]) % NY, (node[1] - parent[1]) % NZ
            partners.add((0, dy, dz, 0))
            partners.add((0, -dy % NY, -dz % NZ, 0))
    barrier = pltpu.get_barrier_semaphore()
    for dx, dy, dz, dc in sorted(partners):
        pl.semaphore_signal(
            barrier, inc=1, device_id=device(dx, dy, dz, dc), device_id_type=MESH
        )
    orb_copy.wait()
    pl.semaphore_wait(barrier, len(partners))

    def remote(src, dst, send, recv, target):
        return pltpu.make_async_remote_copy(
            src_ref=src, dst_ref=dst, send_sem=send, recv_sem=recv,
            device_id=target, device_id_type=MESH,
        )

    inner, leaves = {}, {}
    for c, (_, _, _, kind) in enumerate(chunks):
        edges = plane_tree(kind)
        parents = {parent for _, parent in edges}
        nodes = [node for node, _ in edges if node in parents]
        inner[c] = {node: i for i, node in enumerate(nodes)}
        leaves[c] = len(edges) - len(nodes)

    def share_of(c):
        row, rows, share, _ = chunks[c]
        each = rows // share
        return row, each, (x if share == 4 else lax.rem(x, share))

    def do_node(c, node, kids):
        row, each, part_index = share_of(c)
        table = tables[c]
        block = source(*node)
        if node == (0, 0):
            first = pl.multiple_of(row + part_index * each, 16)
            src = orb.at[pl.ds(first, each)]
        else:
            src = table.at[block]
            remote(
                src, src, plane_send.at[c], root_recv.at[c, inner[c][node]], device(1)
            ).wait_recv()
        for kid in kids:
            recv = (
                root_recv.at[c, inner[c][kid]] if kid in inner[c] else leaf_recv.at[c]
            )
            remote(
                src, table.at[block], plane_send.at[c], recv,
                device(0, kid[0] - node[0], kid[1] - node[1]),
            ).start()
        if node == (0, 0):
            table[block] = orb[pl.ds(first, each)]

    def half_slots(c, part_index, which):
        return lands[c].at[pl.ds(which * (picks // 2), picks // 2), part_index]

    def x_copy(c, part_index, which, recv, dx):
        ref = half_slots(c, part_index, which)
        return remote(ref, ref, x_send.at[c], x_recv.at[c, recv], device(dx))

    def do_select(c):
        _, _, part_index = share_of(c)
        share = chunks[c][2]
        table, land = tables[c], lands[c]
        group = table.at[pl.ds(0, leaves[c])]
        remote(group, group, plane_send.at[c], leaf_recv.at[c], device(1)).wait_recv()
        live = counts[0]
        for s in range(picks):
            picked = table[lists[0, s + 1]]
            land[s, part_index] = jnp.where(s + 1 < live, picked, jnp.zeros_like(picked))
        if share == 4:
            x_copy(c, part_index, 0, 0, 1).start()
            x_copy(c, part_index, 1, 1, -1).start()
            x_copy(c, part_index, 1, 2, 1).start()
            x_copy(c, part_index, 0, 3, -1).start()
        elif share == 2:
            x_copy(c, part_index, 0, 0, 1).start()
            x_copy(c, part_index, 1, 1, -1).start()

    left, right, far = (lax.rem(x + k, NX) for k in (3, 1, 2))

    def do_forward(c):
        x_copy(c, left, 0, 0, 1).wait_recv()
        x_copy(c, left, 0, 4, 1).start()
        x_copy(c, right, 1, 1, -1).wait_recv()
        x_copy(c, right, 1, 5, -1).start()

    def do_arrive(c):
        share = chunks[c][2]
        if share == 4:
            x_copy(c, left, 1, 2, 1).wait_recv()
            x_copy(c, right, 0, 3, 1).wait_recv()
            x_copy(c, far, 0, 4, 1).wait_recv()
            x_copy(c, far, 1, 5, 1).wait_recv()
        elif share == 2:
            theirs_index = lax.rem(x + 1, 2)
            x_copy(c, theirs_index, 0, 0, 1).wait_recv()
            x_copy(c, theirs_index, 1, 1, 1).wait_recv()

    def do_compute(c, p):
        row, rows, _, _ = chunks[c]
        land = lands[c]
        lhs = jnp.concatenate(
            [ints[p, s + 1, :, row : row + rows] for s in range(picks)], axis=1
        )
        rhs = land[...].reshape(picks * rows, orb.shape[1])
        acc[p] += jnp.dot(lhs, rhs, preferred_element_type=F32)

    started = False
    waited = False
    computed = set()
    for event in schedule(chunks):
        what, c = event[1], event[2]
        if what == "node":
            do_node(c, event[3], event[4])
        elif what == "select":
            do_select(c)
        elif what == "forward":
            do_forward(c)
        else:
            if not waited:
                for copy in int_copies[1:]:
                    copy.wait()
                waited = True
            if c not in computed:
                do_arrive(c)
                computed.add(c)
            do_compute(c, event[3])
        if not started:
            started = True
            for copy in int_copies[1:]:
                copy.start()
            int_copies[0].wait()
            for p in range(4):
                acc[p] = jnp.dot(ints[p, 0], orb[...], preferred_element_type=F32)

    width = orb.shape[1]
    for p in range(4):
        half[:, p * width : (p + 1) * width] = acc[p].astype(BF16)

    basis = half.shape[0]
    kept = basis // NX
    sub = kept // 2
    scale = 1.0 / (2 * width)
    order = (2, 1, 3, 0)

    def core_copy(dx):
        return remote(
            part.at[dx, 1 - core], theirs.at[dx], core_send.at[dx], core_recv.at[dx],
            device(dc=1),
        )

    def sum_copy(dx):
        return remote(
            mine.at[dx], arrived.at[dx], sum_send.at[dx], sum_recv.at[dx], device(dx)
        )

    for dx in order:
        target = lax.rem(x + dx, NX)
        rows = half[pl.ds(pl.multiple_of(target * kept, kept), kept)]
        block = lax.dot_general(
            rows, half[...], (((1,), (1,)), ((), ())), preferred_element_type=F32
        )
        part[dx] = (block * scale).reshape(2, sub, basis)
        core_copy(dx).start()
    for dx in order:
        core_copy(dx).wait_recv()
        mine[dx] = part[dx, core] + theirs[dx]
        if dx:
            sum_copy(dx).start()
    total = mine[0]
    for dx in (1, 3, 2):
        sum_copy(dx).wait_recv()
        total = total + arrived[dx]
    mine[0] = total
    last = remote(mine.at[0], other, last_send, last_recv, device(dc=1))
    last.start()
    out_ref[pl.ds(pl.multiple_of(core * sub, sub), sub)] = total
    last.wait_recv()
    out_ref[pl.ds(pl.multiple_of((1 - core) * sub, sub), sub)] = other[...]

    last.wait_send()
    for dx in order:
        core_copy(dx).wait_send()
        if dx:
            sum_copy(dx).wait_send()
    for c, (_, _, share, kind) in enumerate(chunks):
        sent = tables[c].at[pl.ds(0, len(plane_tree(kind)))]
        remote(sent, sent, plane_send.at[c], leaf_recv.at[c], device(1)).wait_send()
        if share == 4:
            sent = lands[c].at[:, pl.ds(0, 3)]
        elif share == 2:
            sent = lands[c].at[:, 0]
        if share > 1:
            remote(sent, sent, x_send.at[c], leaf_recv.at[c], device(1)).wait_send()


def per_device(integrals, orbitals, pair_lists, pair_counts):
    aux, _, slots, basis, _ = integrals.shape
    width = orbitals.shape[1]
    picks = slots - 1
    kept = basis // NX
    count = len(CHUNKS)
    blocks = NY * NZ
    dma = pltpu.SemaphoreType.DMA
    scratch = [
        pltpu.VMEM((aux, slots, basis, basis), BF16),
        pltpu.VMEM((basis, width), BF16),
        pltpu.VMEM((aux, basis, width), F32),
        pltpu.VMEM((basis, aux * width), BF16),
        pltpu.VMEM((NX, 2, kept // 2, basis), F32),
        pltpu.VMEM((NX, kept // 2, basis), F32),
        pltpu.VMEM((NX, kept // 2, basis), F32),
        pltpu.VMEM((NX, kept // 2, basis), F32),
        pltpu.VMEM((kept // 2, basis), F32),
    ]
    scratch += [pltpu.VMEM((blocks, n // g, width), BF16) for _, n, g, _ in CHUNKS]
    scratch += [pltpu.VMEM((picks, g, n // g, width), BF16) for _, n, g, _ in CHUNKS]
    scratch += [
        dma((slots,)), dma, dma((count, 32)), dma((count,)), dma((count,)),
        dma((count, 6)), dma((count,)),
        dma((NX,)), dma((NX,)), dma((NX,)), dma((NX,)), dma, dma,
    ]
    result = pl.pallas_call(
        functools.partial(kernel, CHUNKS),
        out_shape=jax.ShapeDtypeStruct((kept, basis), F32),
        in_specs=[
            pl.BlockSpec(memory_space=pl.ANY),
            pl.BlockSpec(memory_space=pl.ANY),
            pl.BlockSpec(memory_space=pltpu.SMEM),
            pl.BlockSpec(memory_space=pltpu.SMEM),
        ],
        out_specs=pl.BlockSpec(memory_space=pltpu.VMEM),
        scratch_shapes=scratch,
        name="exchange_blocks",
        compiler_params=pltpu.CompilerParams(
            collective_id=0, has_side_effects=True, vmem_limit_bytes=58 * 2**20
        ),
    )(integrals, orbitals, pair_lists, pair_counts)
    return result[None]


def solution(mesh):
    placed = (P("aux", "blk", None, None, None), P("blk", "occ"), P("blk", None), P("blk"))
    return jax.shard_map(
        per_device, mesh=mesh, in_specs=placed, out_specs=P("blk", "aux", None), check_vma=False
    )
```

```python
import functools

import jax
import jax.numpy as jnp
from jax import lax
from jax.experimental import pallas as pl
from jax.experimental.pallas import tpu as pltpu
from jax.sharding import PartitionSpec as P

MESH = pl.DeviceIdType.MESH
NX, NY, NZ = 4, 4, 8
BF16, F32 = jnp.bfloat16, jnp.float32

CHUNKS = (
    (0, 128, 4, "zy quick direct"),
    (128, 64, 4, "yz fwd fwd"),
    (192, 64, 4, "yz fwd fwd"),
    (256, 64, 4, "yz fwd direct"),
    (320, 64, 4, "yz fwd direct"),
    (384, 128, 1, "zy fwd fwd"),
)
GROUPS = ((0, 128), (128, 128), (256, 128), (384, 128))


def z_tree(kind, flip):
    if kind == "direct":
        return [(k, 0) for k in (1, -1, 2, -2, 3, -3, 4)]
    if kind == "quick":
        edges = [(1, 0), (-1, 0), (2, 0), (-2, 0), (3, 2), (-3, -2), (4, 2)]
    else:
        edges = [(1, 0), (-1, 0), (2, 1), (-2, -1), (3, 2), (-3, -2), (4, 3)]
    if flip:
        edges[-1] = (-4, -edges[-1][1])
    return edges


def y_tree(kind, flip):
    if kind == "direct":
        return [(1, 0), (-1, 0), (2, 0)]
    return [(1, 0), (-1, 0), (-2, -1) if flip else (2, 1)]


def plane_tree(kind, flip):
    first, z_kind, y_kind = kind.split()
    edges = []
    if first == "zy":
        for dz, parent in [(0, None)] + z_tree(z_kind, flip):
            if parent is not None:
                edges.append(((0, dz), (0, parent)))
        for dz, _ in [(0, None)] + z_tree(z_kind, flip):
            for dy, parent in y_tree(y_kind, flip ^ (dz & 1)):
                edges.append(((dy, dz), (parent, dz)))
    else:
        for dy, parent in y_tree(y_kind, flip):
            edges.append(((dy, 0), (parent, 0)))
        for dy, _ in [(0, None)] + y_tree(y_kind, flip):
            for dz, parent in z_tree(z_kind, flip ^ (dy & 1)):
                edges.append(((dy, dz), (dy, parent)))
    return edges


def hop_counts(node, parent):
    return node[0] - parent[0], node[1] - parent[1]


LINK = 0.011
ISSUE, FIXED, HOP = 0.05, 1.4, 0.65
PRODUCT = 1.2


def schedule(chunks):
    free = {}
    clock = 0.0
    pending = []
    arrived = {}
    waiting = [depth for _, depth in GROUPS]

    def send(way, hops, kib):
        nonlocal clock
        clock += ISSUE
        if abs(hops) == 2 and way == "y":
            ways, load = (("y", 1), ("y", -1)), 1.0
        else:
            ways, load = ((way, 1 if hops > 0 else -1),), abs(hops)
        begin = max([clock] + [free.get(w, 0.0) for w in ways])
        end = begin + load * 2 * kib * LINK
        for w in ways:
            free[w] = end
        return end + FIXED + HOP * abs(hops)

    trees = []
    for c, (row, rows, share, kind) in enumerate(chunks):
        edges = plane_tree(kind, c & 1)
        kids = {}
        for node, parent in edges:
            kids.setdefault(parent, []).append(node)
        trees.append((kids, len(edges)))
        pending.append((0.25 * c, c, ("node", c, (0, 0))))
    left = [n for _, n in trees]
    latest = [0.0] * len(chunks)
    order = []
    while pending:
        early = [e for e in pending if e[0] <= clock]
        pick = (
            min(early, key=lambda e: (e[2][0] == "compute", e[1], e[0]))
            if early
            else min(pending)
        )
        pending.remove(pick)
        clock = max(clock, pick[0]) + 0.03
        event = pick[2]
        what, c = event[0], event[1]
        if what == "compute":
            order.append(event)
            clock += PRODUCT * GROUPS[c][1] / 128 + 0.4
            continue
        row, rows, share, kind = chunks[c]
        each = rows // share
        kib = each / 2
        if what == "node":
            kids, _ = trees[c]
            nodes = kids[event[2]]
            order.append(("node", c, event[2], tuple(nodes)))
            for kid in nodes:
                dy, dz = hop_counts(kid, event[2])
                t = send("y", dy, kib) if dy else send("z", dz, kib)
                latest[c] = max(latest[c], t)
                left[c] -= 1
                if kid in kids:
                    pending.append((t, c, ("node", c, kid)))
            if left[c] == 0:
                pending.append((latest[c], c, ("select", c)))
        elif what == "select":
            order.append(event)
            clock += 0.1 + 0.004 * each
            if share == 4:
                t1, t2 = send("x", 1, 5 * kib), send("x", -1, 5 * kib)
                t3, t4 = send("x", 1, 5 * kib), send("x", -1, 5 * kib)
                arrived[c] = max(t3, t4)
                pending.append((max(t1, t2), c, ("forward", c)))
            elif share == 2:
                ready = max(send("x", 1, 5 * kib), send("x", -1, 5 * kib))
                pending.append((ready, c, ("arrive", c)))
            else:
                pending.append((clock, c, ("arrive", c)))
        elif what == "forward":
            order.append(event)
            ready = max(send("x", 1, 5 * kib), send("x", -1, 5 * kib), arrived[c])
            pending.append((ready, c, ("arrive", c)))
        else:
            order.append(event)
            for g, (first, depth) in enumerate(GROUPS):
                if first <= row < first + depth:
                    waiting[g] -= rows
                    if waiting[g] == 0:
                        pending.append((clock, g, ("compute", g)))
    return order, clock


def kernel(
    chunks, ints_hbm, orb_hbm, lists_hbm, counts_hbm, out_ref,
    ints, orb, acc, half, part, theirs, mine, arrived, other, *refs,
):
    count = len(chunks)
    tables, land = refs[:count], refs[count]
    (
        lists, counts, list_sem, int_sem, orb_sem, root_recv, leaf_recv, plane_send, x_recv, x_send,
        core_send, core_recv, sum_send, sum_recv, last_send, last_recv,
    ) = refs[count + 1 :]
    slots = ints.shape[1]
    picks = slots - 1
    x = lax.axis_index("aux")
    plane = lax.axis_index("blk")
    core = lax.axis_index("occ")
    y, z = lax.rem(plane, NY), plane // NY

    def device(dx=0, dy=0, dz=0, dc=0):
        return (
            lax.rem(x + (dx + NX), NX),
            lax.rem(z + (dz + NZ), NZ) * NY + lax.rem(y + (dy + NY), NY),
            lax.rem(core + dc, 2),
        )

    def source(dy, dz):
        return lax.rem(z + (NZ - dz), NZ) * NY + lax.rem(y + (NY - dy), NY)

    int_copies = [
        pltpu.make_async_copy(ints_hbm.at[:, 0, 0], ints.at[:, 0], int_sem.at[0])
    ]
    for c, (row, rows) in enumerate(GROUPS):
        int_copies.append(
            pltpu.make_async_copy(
                ints_hbm.at[:, 0, pl.ds(1, slots - 1), :, pl.ds(row, rows)],
                ints.at[:, pl.ds(1, slots - 1), :, pl.ds(row, rows)],
                int_sem.at[c + 1],
            )
        )
    orb_copy = pltpu.make_async_copy(orb_hbm, orb, orb_sem)
    list_copies = (
        pltpu.make_async_copy(lists_hbm, lists, list_sem.at[0]),
        pltpu.make_async_copy(counts_hbm, counts, list_sem.at[1]),
    )
    orb_copy.start()
    for copy in list_copies:
        copy.start()
    int_copies[0].start()

    partners = {(1, 0, 0, 0), (3, 0, 0, 0), (2, 0, 0, 0), (0, 0, 0, 1)}
    for c, (_, _, _, kind) in enumerate(chunks):
        for node, parent in plane_tree(kind, c & 1):
            dy, dz = (node[0] - parent[0]) % NY, (node[1] - parent[1]) % NZ
            partners.add((0, dy, dz, 0))
            partners.add((0, -dy % NY, -dz % NZ, 0))
    barrier = pltpu.get_barrier_semaphore()
    for dx, dy, dz, dc in sorted(partners):
        pl.semaphore_signal(
            barrier, inc=1, device_id=device(dx, dy, dz, dc), device_id_type=MESH
        )
    orb_copy.wait()
    for copy in list_copies:
        copy.wait()
    pl.semaphore_wait(barrier, len(partners))

    def remote(src, dst, send, recv, target):
        return pltpu.make_async_remote_copy(
            src_ref=src, dst_ref=dst, send_sem=send, recv_sem=recv,
            device_id=target, device_id_type=MESH,
        )

    inner, leaves = {}, {}
    for c, (_, _, _, kind) in enumerate(chunks):
        edges = plane_tree(kind, c & 1)
        parents = {parent for _, parent in edges}
        nodes = [node for node, _ in edges if node in parents]
        inner[c] = {node: i for i, node in enumerate(nodes)}
        leaves[c] = len(edges) - len(nodes)

    def share_of(c):
        row, rows, share, _ = chunks[c]
        each = rows // share
        return row, each, (x if share == 4 else lax.rem(x, share))

    def do_node(c, node, kids):
        row, each, part_index = share_of(c)
        table = tables[c]
        block = source(*node)
        if node == (0, 0):
            first = pl.multiple_of(row + part_index * each, 16)
            src = orb.at[pl.ds(first, each)]
        else:
            src = table.at[block]
            remote(
                src, src, plane_send.at[c], root_recv.at[c, inner[c][node]], device(1)
            ).wait_recv()
        for kid in kids:
            recv = (
                root_recv.at[c, inner[c][kid]] if kid in inner[c] else leaf_recv.at[c]
            )
            remote(
                src, table.at[block], plane_send.at[c], recv,
                device(0, kid[0] - node[0], kid[1] - node[1]),
            ).start()
        if node == (0, 0):
            table[block] = orb[pl.ds(first, each)]

    def own_rows(c, part_index):
        row, each, _ = share_of(c)
        return pl.ds(pl.multiple_of(row + part_index * each, 16), each)

    def half_slots(c, part_index, which):
        return land.at[
            pl.ds(which * (picks // 2), picks // 2), own_rows(c, part_index)
        ]

    def x_copy(c, part_index, which, recv, dx):
        ref = half_slots(c, part_index, which)
        return remote(ref, ref, x_send.at[c], x_recv.at[c, recv], device(dx))

    def do_select(c):
        _, _, part_index = share_of(c)
        share = chunks[c][2]
        table, here = tables[c], own_rows(c, part_index)
        group = table.at[pl.ds(0, leaves[c])]
        remote(group, group, plane_send.at[c], leaf_recv.at[c], device(1)).wait_recv()
        live = counts[0]
        for s in range(picks):
            picked = table[lists[0, s + 1]]
            land[s, here] = jnp.where(s + 1 < live, picked, jnp.zeros_like(picked))
        if share == 4:
            x_copy(c, part_index, 0, 0, 1).start()
            x_copy(c, part_index, 1, 1, -1).start()
            x_copy(c, part_index, 1, 2, 1).start()
            x_copy(c, part_index, 0, 3, -1).start()
        elif share == 2:
            x_copy(c, part_index, 0, 0, 1).start()
            x_copy(c, part_index, 1, 1, -1).start()

    left, right, far = (lax.rem(x + k, NX) for k in (3, 1, 2))

    def do_forward(c):
        x_copy(c, left, 0, 0, 1).wait_recv()
        x_copy(c, left, 0, 4, 1).start()
        x_copy(c, right, 1, 1, -1).wait_recv()
        x_copy(c, right, 1, 5, -1).start()

    def do_arrive(c):
        share = chunks[c][2]
        if share == 4:
            x_copy(c, left, 1, 2, 1).wait_recv()
            x_copy(c, right, 0, 3, 1).wait_recv()
            x_copy(c, far, 0, 4, 1).wait_recv()
            x_copy(c, far, 1, 5, 1).wait_recv()
        elif share == 2:
            theirs_index = lax.rem(x + 1, 2)
            x_copy(c, theirs_index, 0, 0, 1).wait_recv()
            x_copy(c, theirs_index, 1, 1, 1).wait_recv()

    def product(g, p):
        row, rows = GROUPS[g]
        lhs = jnp.concatenate(
            [ints[p, s + 1, :, row : row + rows] for s in range(picks)], axis=1
        )
        rhs = land[:, row : row + rows].reshape(picks * rows, orb.shape[1])
        return acc[p] + jnp.dot(lhs, rhs, preferred_element_type=F32)

    order, _ = schedule(chunks)
    started = False
    for event in order:
        what, c = event[0], event[1]
        if what == "node":
            do_node(c, event[2], event[3])
        elif what == "select":
            do_select(c)
        elif what == "forward":
            do_forward(c)
        elif what == "arrive":
            do_arrive(c)
        else:
            int_copies[c + 1].wait()
            if event is not order[-1]:
                for p in range(4):
                    acc[p] = product(c, p)
        if not started:
            started = True
            for copy in int_copies[1:]:
                copy.start()
            int_copies[0].wait()
            for p in range(4):
                acc[p] = jnp.dot(ints[p, 0], orb[...], preferred_element_type=F32)

    width = orb.shape[1]
    final = order[-1][1]
    for p in range(4):
        half[:, p * width : (p + 1) * width] = product(final, p).astype(BF16)

    basis = half.shape[0]
    kept = basis // NX
    sub = kept // 2
    scale = 1.0 / (2 * width)
    block = lax.dot_general(
        half[...], half[...], (((1,), (1,)), ((), ())), preferred_element_type=F32
    )
    part[...] = (block * scale).reshape(NX, 2, sub, basis)
    order = (2, 1, 3, 0)
    targets = [lax.rem(x + dx, NX) for dx in range(NX)]

    def core_copy(dx):
        return remote(
            part.at[targets[dx], 1 - core], theirs.at[dx], core_send.at[dx], core_recv.at[dx],
            device(dc=1),
        )

    def sum_copy(dx):
        return remote(
            mine.at[dx], arrived.at[dx], sum_send.at[dx], sum_recv.at[dx], device(dx)
        )

    for dx in order:
        core_copy(dx).start()
    for dx in order:
        core_copy(dx).wait_recv()
        mine[dx] = part[targets[dx], core] + theirs[dx]
        if dx:
            sum_copy(dx).start()
    total = mine[0]
    for dx in (1, 3, 2):
        sum_copy(dx).wait_recv()
        total = total + arrived[dx]
    mine[0] = total
    last = remote(mine.at[0], other, last_send, last_recv, device(dc=1))
    last.start()
    out_ref[pl.ds(pl.multiple_of(core * sub, sub), sub)] = total
    last.wait_recv()
    out_ref[pl.ds(pl.multiple_of((1 - core) * sub, sub), sub)] = other[...]

    last.wait_send()
    for dx in order:
        core_copy(dx).wait_send()
        if dx:
            sum_copy(dx).wait_send()
    for c, (_, _, share, kind) in enumerate(chunks):
        sent = tables[c].at[pl.ds(0, len(plane_tree(kind, c & 1)))]
        remote(sent, sent, plane_send.at[c], leaf_recv.at[c], device(1)).wait_send()
        if share == 4:
            sent = land.at[:, pl.ds(0, 3 * share_of(c)[1])]
        elif share == 2:
            sent = land.at[:, pl.ds(0, share_of(c)[1])]
        if share > 1:
            remote(sent, sent, x_send.at[c], leaf_recv.at[c], device(1)).wait_send()


def per_device(integrals, orbitals, pair_lists, pair_counts):
    aux, _, slots, basis, _ = integrals.shape
    width = orbitals.shape[1]
    picks = slots - 1
    kept = basis // NX
    count = len(CHUNKS)
    blocks = NY * NZ
    dma = pltpu.SemaphoreType.DMA
    scratch = [
        pltpu.VMEM((aux, slots, basis, basis), BF16),
        pltpu.VMEM((basis, width), BF16),
        pltpu.VMEM((aux, basis, width), F32),
        pltpu.VMEM((basis, aux * width), BF16),
        pltpu.VMEM((NX, 2, kept // 2, basis), F32),
        pltpu.VMEM((NX, kept // 2, basis), F32),
        pltpu.VMEM((NX, kept // 2, basis), F32),
        pltpu.VMEM((NX, kept // 2, basis), F32),
        pltpu.VMEM((kept // 2, basis), F32),
    ]
    scratch += [pltpu.VMEM((blocks, n // g, width), BF16) for _, n, g, _ in CHUNKS]
    scratch += [pltpu.VMEM((picks, basis, width), BF16)]
    scratch += [
        pltpu.SMEM((1, slots), jnp.int32), pltpu.SMEM((1,), jnp.int32), dma((2,)),
        dma((len(GROUPS) + 1,)), dma, dma((count, 32)), dma((count,)), dma((count,)),
        dma((count, 6)), dma((count,)),
        dma((NX,)), dma((NX,)), dma((NX,)), dma((NX,)), dma, dma,
    ]
    result = pl.pallas_call(
        functools.partial(kernel, CHUNKS),
        out_shape=jax.ShapeDtypeStruct((kept, basis), F32),
        in_specs=[
            pl.BlockSpec(memory_space=pl.ANY),
            pl.BlockSpec(memory_space=pl.ANY),
            pl.BlockSpec(memory_space=pl.ANY),
            pl.BlockSpec(memory_space=pl.ANY),
        ],
        out_specs=pl.BlockSpec(memory_space=pltpu.VMEM),
        scratch_shapes=scratch,
        name="exchange_blocks",
        compiler_params=pltpu.CompilerParams(
            collective_id=0, has_side_effects=True, vmem_limit_bytes=42 * 2**20
        ),
    )(integrals, orbitals, pair_lists, pair_counts)
    return result[None]


def solution(mesh):
    placed = (P("aux", "blk", None, None, None), P("blk", "occ"), P("blk", None), P("blk"))
    return jax.shard_map(
        per_device, mesh=mesh, in_specs=placed, out_specs=P("blk", "aux", None), check_vma=False
    )
```

```python
import functools

import jax
import jax.numpy as jnp
from jax import lax
from jax.experimental import pallas as pl
from jax.experimental.pallas import tpu as pltpu
from jax.sharding import PartitionSpec as P

MESH = pl.DeviceIdType.MESH
NX, NY, NZ = 4, 4, 8
BF16, F32 = jnp.bfloat16, jnp.float32

CHUNKS = (
    (0, 128, 4, "zy quick direct"),
    (128, 64, 4, "yz fwd fwd"),
    (192, 64, 4, "yz fwd fwd"),
    (256, 64, 4, "yz fwd direct"),
    (320, 64, 4, "yz fwd direct"),
    (384, 128, 1, "zy fwd fwd"),
)
GROUPS = ((0, 128), (128, 128), (256, 128), (384, 128))


def z_tree(kind, flip):
    if kind == "direct":
        return [(k, 0) for k in (1, -1, 2, -2, 3, -3, 4)]
    if kind == "quick":
        edges = [(1, 0), (-1, 0), (2, 0), (-2, 0), (3, 2), (-3, -2), (4, 2)]
    else:
        edges = [(1, 0), (-1, 0), (2, 1), (-2, -1), (3, 2), (-3, -2), (4, 3)]
    if flip:
        edges[-1] = (-4, -edges[-1][1])
    return edges


def y_tree(kind, flip):
    if kind == "direct":
        return [(1, 0), (-1, 0), (2, 0)]
    return [(1, 0), (-1, 0), (-2, -1) if flip else (2, 1)]


def plane_tree(kind, flip):
    first, z_kind, y_kind = kind.split()
    edges = []
    if first == "zy":
        for dz, parent in [(0, None)] + z_tree(z_kind, flip):
            if parent is not None:
                edges.append(((0, dz), (0, parent)))
        for dz, _ in [(0, None)] + z_tree(z_kind, flip):
            for dy, parent in y_tree(y_kind, flip ^ (dz & 1)):
                edges.append(((dy, dz), (parent, dz)))
    else:
        for dy, parent in y_tree(y_kind, flip):
            edges.append(((dy, 0), (parent, 0)))
        for dy, _ in [(0, None)] + y_tree(y_kind, flip):
            for dz, parent in z_tree(z_kind, flip ^ (dy & 1)):
                edges.append(((dy, dz), (dy, parent)))
    return edges


def hop_counts(node, parent):
    return node[0] - parent[0], node[1] - parent[1]


LINK = 0.011
ISSUE, FIXED, HOP = 0.05, 1.4, 0.65
PRODUCT = 1.2


def schedule(chunks):
    free = {}
    clock = 0.0
    pending = []
    arrived = {}
    waiting = [depth for _, depth in GROUPS]

    def send(way, hops, kib):
        nonlocal clock
        clock += ISSUE
        if abs(hops) == 2 and way == "y":
            ways, load = (("y", 1), ("y", -1)), 1.0
        else:
            ways, load = ((way, 1 if hops > 0 else -1),), abs(hops)
        begin = max([clock] + [free.get(w, 0.0) for w in ways])
        end = begin + load * 2 * kib * LINK
        for w in ways:
            free[w] = end
        return end + FIXED + HOP * abs(hops)

    trees = []
    for c, (row, rows, share, kind) in enumerate(chunks):
        edges = plane_tree(kind, c & 1)
        kids = {}
        for node, parent in edges:
            kids.setdefault(parent, []).append(node)
        trees.append((kids, len(edges)))
        pending.append((0.25 * c, c, ("node", c, (0, 0))))
    left = [n for _, n in trees]
    latest = [0.0] * len(chunks)
    order = []
    while pending:
        early = [e for e in pending if e[0] <= clock]
        pick = (
            min(early, key=lambda e: (e[2][0] == "compute", e[1], e[0]))
            if early
            else min(pending)
        )
        pending.remove(pick)
        clock = max(clock, pick[0]) + 0.03
        event = pick[2]
        what, c = event[0], event[1]
        if what == "compute":
            order.append(event)
            clock += PRODUCT * GROUPS[c][1] / 128 + 0.4
            continue
        row, rows, share, kind = chunks[c]
        each = rows // share
        kib = each / 2
        if what == "node":
            kids, _ = trees[c]
            nodes = kids[event[2]]
            order.append(("node", c, event[2], tuple(nodes)))
            for kid in nodes:
                dy, dz = hop_counts(kid, event[2])
                t = send("y", dy, kib) if dy else send("z", dz, kib)
                latest[c] = max(latest[c], t)
                left[c] -= 1
                if kid in kids:
                    pending.append((t, c, ("node", c, kid)))
            if left[c] == 0:
                pending.append((latest[c], c, ("select", c)))
        elif what == "select":
            order.append(event)
            clock += 0.1 + 0.004 * each
            if share == 4:
                t1, t2 = send("x", 1, 5 * kib), send("x", -1, 5 * kib)
                t3, t4 = send("x", 1, 5 * kib), send("x", -1, 5 * kib)
                arrived[c] = max(t3, t4)
                pending.append((max(t1, t2), c, ("forward", c)))
            elif share == 2:
                ready = max(send("x", 1, 5 * kib), send("x", -1, 5 * kib))
                pending.append((ready, c, ("arrive", c)))
            else:
                pending.append((clock, c, ("arrive", c)))
        elif what == "forward":
            order.append(event)
            ready = max(send("x", 1, 5 * kib), send("x", -1, 5 * kib), arrived[c])
            pending.append((ready, c, ("arrive", c)))
        else:
            order.append(event)
            for g, (first, depth) in enumerate(GROUPS):
                if first <= row < first + depth:
                    waiting[g] -= rows
                    if waiting[g] == 0:
                        pending.append((clock, g, ("compute", g)))
    return order, clock


def kernel(
    chunks, ints_hbm, orb_hbm, lists_hbm, counts_hbm, out_ref,
    ints, orb, acc, half, part, theirs, mine, coded, steps, other, *refs,
):
    count = len(chunks)
    tables, land = refs[:count], refs[count]
    (
        lists, counts, list_sem, int_sem, orb_sem, root_recv, leaf_recv, plane_send, x_recv, x_send,
        core_send, core_recv, sum_send, sum_recv, step_send, step_recv, last_send, last_recv,
    ) = refs[count + 1 :]
    slots = ints.shape[1]
    picks = slots - 1
    x = lax.axis_index("aux")
    plane = lax.axis_index("blk")
    core = lax.axis_index("occ")
    y, z = lax.rem(plane, NY), plane // NY

    def device(dx=0, dy=0, dz=0, dc=0):
        return (
            lax.rem(x + (dx + NX), NX),
            lax.rem(z + (dz + NZ), NZ) * NY + lax.rem(y + (dy + NY), NY),
            lax.rem(core + dc, 2),
        )

    def source(dy, dz):
        return lax.rem(z + (NZ - dz), NZ) * NY + lax.rem(y + (NY - dy), NY)

    int_copies = [
        pltpu.make_async_copy(ints_hbm.at[:, 0, 0], ints.at[:, 0], int_sem.at[0])
    ]
    for c, (row, rows) in enumerate(GROUPS):
        int_copies.append(
            pltpu.make_async_copy(
                ints_hbm.at[:, 0, pl.ds(1, slots - 1), :, pl.ds(row, rows)],
                ints.at[:, pl.ds(1, slots - 1), :, pl.ds(row, rows)],
                int_sem.at[c + 1],
            )
        )
    orb_copy = pltpu.make_async_copy(orb_hbm, orb, orb_sem)
    list_copies = (
        pltpu.make_async_copy(lists_hbm, lists, list_sem.at[0]),
        pltpu.make_async_copy(counts_hbm, counts, list_sem.at[1]),
    )
    orb_copy.start()
    for copy in list_copies:
        copy.start()
    int_copies[0].start()

    partners = {(1, 0, 0, 0), (3, 0, 0, 0), (2, 0, 0, 0), (0, 0, 0, 1)}
    for c, (_, _, _, kind) in enumerate(chunks):
        for node, parent in plane_tree(kind, c & 1):
            dy, dz = (node[0] - parent[0]) % NY, (node[1] - parent[1]) % NZ
            partners.add((0, dy, dz, 0))
            partners.add((0, -dy % NY, -dz % NZ, 0))
    barrier = pltpu.get_barrier_semaphore()
    for dx, dy, dz, dc in sorted(partners):
        pl.semaphore_signal(
            barrier, inc=1, device_id=device(dx, dy, dz, dc), device_id_type=MESH
        )
    orb_copy.wait()
    for copy in list_copies:
        copy.wait()
    pl.semaphore_wait(barrier, len(partners))

    def remote(src, dst, send, recv, target):
        return pltpu.make_async_remote_copy(
            src_ref=src, dst_ref=dst, send_sem=send, recv_sem=recv,
            device_id=target, device_id_type=MESH,
        )

    inner, leaves = {}, {}
    for c, (_, _, _, kind) in enumerate(chunks):
        edges = plane_tree(kind, c & 1)
        parents = {parent for _, parent in edges}
        nodes = [node for node, _ in edges if node in parents]
        inner[c] = {node: i for i, node in enumerate(nodes)}
        leaves[c] = len(edges) - len(nodes)

    def share_of(c):
        row, rows, share, _ = chunks[c]
        each = rows // share
        return row, each, (x if share == 4 else lax.rem(x, share))

    def do_node(c, node, kids):
        row, each, part_index = share_of(c)
        table = tables[c]
        block = source(*node)
        if node == (0, 0):
            first = pl.multiple_of(row + part_index * each, 16)
            src = orb.at[pl.ds(first, each)]
        else:
            src = table.at[block]
            remote(
                src, src, plane_send.at[c], root_recv.at[c, inner[c][node]], device(1)
            ).wait_recv()
        for kid in kids:
            recv = (
                root_recv.at[c, inner[c][kid]] if kid in inner[c] else leaf_recv.at[c]
            )
            remote(
                src, table.at[block], plane_send.at[c], recv,
                device(0, kid[0] - node[0], kid[1] - node[1]),
            ).start()
        if node == (0, 0):
            table[block] = orb[pl.ds(first, each)]

    def own_rows(c, part_index):
        row, each, _ = share_of(c)
        return pl.ds(pl.multiple_of(row + part_index * each, 16), each)

    def half_slots(c, part_index, which):
        return land.at[
            pl.ds(which * (picks // 2), picks // 2), own_rows(c, part_index)
        ]

    def x_copy(c, part_index, which, recv, dx):
        ref = half_slots(c, part_index, which)
        return remote(ref, ref, x_send.at[c], x_recv.at[c, recv], device(dx))

    def do_select(c):
        _, _, part_index = share_of(c)
        share = chunks[c][2]
        table, here = tables[c], own_rows(c, part_index)
        group = table.at[pl.ds(0, leaves[c])]
        remote(group, group, plane_send.at[c], leaf_recv.at[c], device(1)).wait_recv()
        live = counts[0]
        for s in range(picks):
            picked = table[lists[0, s + 1]]
            land[s, here] = jnp.where(s + 1 < live, picked, jnp.zeros_like(picked))
        if share == 4:
            x_copy(c, part_index, 0, 0, 1).start()
            x_copy(c, part_index, 1, 1, -1).start()
            x_copy(c, part_index, 1, 2, 1).start()
            x_copy(c, part_index, 0, 3, -1).start()
        elif share == 2:
            x_copy(c, part_index, 0, 0, 1).start()
            x_copy(c, part_index, 1, 1, -1).start()

    left, right, far = (lax.rem(x + k, NX) for k in (3, 1, 2))

    def do_forward(c):
        x_copy(c, left, 0, 0, 1).wait_recv()
        x_copy(c, left, 0, 4, 1).start()
        x_copy(c, right, 1, 1, -1).wait_recv()
        x_copy(c, right, 1, 5, -1).start()

    def do_arrive(c):
        share = chunks[c][2]
        if share == 4:
            x_copy(c, left, 1, 2, 1).wait_recv()
            x_copy(c, right, 0, 3, 1).wait_recv()
            x_copy(c, far, 0, 4, 1).wait_recv()
            x_copy(c, far, 1, 5, 1).wait_recv()
        elif share == 2:
            theirs_index = lax.rem(x + 1, 2)
            x_copy(c, theirs_index, 0, 0, 1).wait_recv()
            x_copy(c, theirs_index, 1, 1, 1).wait_recv()

    def product(g, p):
        row, rows = GROUPS[g]
        lhs = jnp.concatenate(
            [ints[p, s + 1, :, row : row + rows] for s in range(picks)], axis=1
        )
        rhs = land[:, row : row + rows].reshape(picks * rows, orb.shape[1])
        return acc[p] + jnp.dot(lhs, rhs, preferred_element_type=F32)

    order, _ = schedule(chunks)
    started = False
    for event in order:
        what, c = event[0], event[1]
        if what == "node":
            do_node(c, event[2], event[3])
        elif what == "select":
            do_select(c)
        elif what == "forward":
            do_forward(c)
        elif what == "arrive":
            do_arrive(c)
        else:
            int_copies[c + 1].wait()
            if event is not order[-1]:
                for p in range(4):
                    acc[p] = product(c, p)
        if not started:
            started = True
            for copy in int_copies[1:]:
                copy.start()
            int_copies[0].wait()
            for p in range(4):
                acc[p] = jnp.dot(ints[p, 0], orb[...], preferred_element_type=F32)

    width = orb.shape[1]
    final = order[-1][1]
    for p in range(4):
        half[:, p * width : (p + 1) * width] = product(final, p).astype(BF16)

    basis = half.shape[0]
    kept = basis // NX
    sub = kept // 2
    scale = 1.0 / (2 * width)
    block = lax.dot_general(
        half[...], half[...], (((1,), (1,)), ((), ())), preferred_element_type=F32
    )
    part[...] = (block * scale).reshape(NX, 2, sub, basis)
    order = (2, 1, 3, 0)
    targets = [lax.rem(x + dx, NX) for dx in range(NX)]

    def core_copy(dx):
        return remote(
            part.at[targets[dx], 1 - core], theirs.at[dx], core_send.at[dx], core_recv.at[dx],
            device(dc=1),
        )

    def sum_copies(dx):
        return (
            remote(
                steps.at[dx, 0], steps.at[dx, 1], step_send.at[dx], step_recv.at[dx],
                device(dx),
            ),
            remote(
                coded.at[dx, 0], coded.at[dx, 1], sum_send.at[dx], sum_recv.at[dx],
                device(dx),
            ),
        )

    def encode(dx, value):
        parts = []
        for g in range(sub // 8):
            rows = value[8 * g : 8 * g + 8]
            top = jnp.max(jnp.abs(rows), axis=(0, 1), keepdims=True)
            step = jnp.maximum(top, 1e-33) * (1.0 / 32000.0)
            steps[dx, 0, g : g + 1] = jnp.broadcast_to(step, (1, 128))
            parts.append(jnp.round(rows * (1.0 / step)).astype(jnp.int32))
        coded[dx, 0] = jnp.concatenate(parts, axis=0).astype(jnp.int16)

    def decode(dx):
        whole = coded[dx, 1].astype(jnp.int32).astype(F32)
        size = steps[dx, 1]
        return jnp.concatenate(
            [
                whole[8 * g : 8 * g + 8] * size[g : g + 1, 0:1]
                for g in range(sub // 8)
            ],
            axis=0,
        )

    for dx in order:
        core_copy(dx).start()
    for dx in order:
        core_copy(dx).wait_recv()
        chip_sum = part[targets[dx], core] + theirs[dx]
        if dx:
            encode(dx, chip_sum)
            for copy in sum_copies(dx):
                copy.start()
    total = chip_sum
    for dx in (1, 3, 2):
        for copy in sum_copies(dx):
            copy.wait_recv()
        total = total + decode(dx)
    mine[...] = total
    last = remote(mine, other, last_send, last_recv, device(dc=1))
    last.start()
    out_ref[pl.ds(pl.multiple_of(core * sub, sub), sub)] = total
    last.wait_recv()
    out_ref[pl.ds(pl.multiple_of((1 - core) * sub, sub), sub)] = other[...]

    last.wait_send()
    for dx in order:
        core_copy(dx).wait_send()
        if dx:
            for copy in sum_copies(dx):
                copy.wait_send()
    for c, (_, _, share, kind) in enumerate(chunks):
        sent = tables[c].at[pl.ds(0, len(plane_tree(kind, c & 1)))]
        remote(sent, sent, plane_send.at[c], leaf_recv.at[c], device(1)).wait_send()
        if share == 4:
            sent = land.at[:, pl.ds(0, 3 * share_of(c)[1])]
        elif share == 2:
            sent = land.at[:, pl.ds(0, share_of(c)[1])]
        if share > 1:
            remote(sent, sent, x_send.at[c], leaf_recv.at[c], device(1)).wait_send()


def per_device(integrals, orbitals, pair_lists, pair_counts):
    aux, _, slots, basis, _ = integrals.shape
    width = orbitals.shape[1]
    picks = slots - 1
    kept = basis // NX
    count = len(CHUNKS)
    blocks = NY * NZ
    dma = pltpu.SemaphoreType.DMA
    scratch = [
        pltpu.VMEM((aux, slots, basis, basis), BF16),
        pltpu.VMEM((basis, width), BF16),
        pltpu.VMEM((aux, basis, width), F32),
        pltpu.VMEM((basis, aux * width), BF16),
        pltpu.VMEM((NX, 2, kept // 2, basis), F32),
        pltpu.VMEM((NX, kept // 2, basis), F32),
        pltpu.VMEM((kept // 2, basis), F32),
        pltpu.VMEM((NX, 2, kept // 2, basis), jnp.int16),
        pltpu.VMEM((NX, 2, kept // 16, 128), F32),
        pltpu.VMEM((kept // 2, basis), F32),
    ]
    scratch += [pltpu.VMEM((blocks, n // g, width), BF16) for _, n, g, _ in CHUNKS]
    scratch += [pltpu.VMEM((picks, basis, width), BF16)]
    scratch += [
        pltpu.SMEM((1, slots), jnp.int32), pltpu.SMEM((1,), jnp.int32), dma((2,)),
        dma((len(GROUPS) + 1,)), dma, dma((count, 32)), dma((count,)), dma((count,)),
        dma((count, 6)), dma((count,)),
        dma((NX,)), dma((NX,)), dma((NX,)), dma((NX,)), dma((NX,)), dma((NX,)), dma, dma,
    ]
    result = pl.pallas_call(
        functools.partial(kernel, CHUNKS),
        out_shape=jax.ShapeDtypeStruct((kept, basis), F32),
        in_specs=[
            pl.BlockSpec(memory_space=pl.ANY),
            pl.BlockSpec(memory_space=pl.ANY),
            pl.BlockSpec(memory_space=pl.ANY),
            pl.BlockSpec(memory_space=pl.ANY),
        ],
        out_specs=pl.BlockSpec(memory_space=pltpu.VMEM),
        scratch_shapes=scratch,
        name="exchange_blocks",
        compiler_params=pltpu.CompilerParams(
            collective_id=0, has_side_effects=True, vmem_limit_bytes=42 * 2**20
        ),
    )(integrals, orbitals, pair_lists, pair_counts)
    return result[None]


def solution(mesh):
    placed = (P("aux", "blk", None, None, None), P("blk", "occ"), P("blk", None), P("blk"))
    return jax.shard_map(
        per_device, mesh=mesh, in_specs=placed, out_specs=P("blk", "aux", None), check_vma=False
    )
```

```python
import functools

import jax
import jax.numpy as jnp
from jax import lax
from jax.experimental import pallas as pl
from jax.experimental.pallas import tpu as pltpu
from jax.sharding import PartitionSpec as P

MESH = pl.DeviceIdType.MESH
NX, NY, NZ = 4, 4, 8
BF16, F32 = jnp.bfloat16, jnp.float32

CHUNKS = (
    (0, 128, 4, "zy quick direct"),
    (128, 128, 4, "yz fwd fwd"),
    (256, 128, 4, "yz fwd direct"),
    (384, 128, 1, "zy fwd fwd"),
)
GROUPS = ((0, 128), (128, 128), (256, 128), (384, 128))


def z_tree(kind, flip):
    if kind == "direct":
        return [(k, 0) for k in (1, -1, 2, -2, 3, -3, 4)]
    if kind == "quick":
        edges = [(1, 0), (-1, 0), (2, 0), (-2, 0), (3, 2), (-3, -2), (4, 2)]
    else:
        edges = [(1, 0), (-1, 0), (2, 1), (-2, -1), (3, 2), (-3, -2), (4, 3)]
    if flip:
        edges[-1] = (-4, -edges[-1][1])
    return edges


def y_tree(kind, flip):
    if kind == "direct":
        return [(1, 0), (-1, 0), (2, 0)]
    return [(1, 0), (-1, 0), (-2, -1) if flip else (2, 1)]


def plane_tree(kind, flip):
    first, z_kind, y_kind = kind.split()
    edges = []
    if first == "zy":
        for dz, parent in [(0, None)] + z_tree(z_kind, flip):
            if parent is not None:
                edges.append(((0, dz), (0, parent)))
        for dz, _ in [(0, None)] + z_tree(z_kind, flip):
            for dy, parent in y_tree(y_kind, flip ^ (dz & 1)):
                edges.append(((dy, dz), (parent, dz)))
    else:
        for dy, parent in y_tree(y_kind, flip):
            edges.append(((dy, 0), (parent, 0)))
        for dy, _ in [(0, None)] + y_tree(y_kind, flip):
            for dz, parent in z_tree(z_kind, flip ^ (dy & 1)):
                edges.append(((dy, dz), (dy, parent)))
    return edges


def hop_counts(node, parent):
    return node[0] - parent[0], node[1] - parent[1]


LINK = 0.01
ISSUE, FIXED, HOP = 0.04, 1.8, 0.65
PRODUCT = 1.2


def schedule(chunks):
    free = {}
    clock = 0.0
    pending = []
    arrived = {}
    waiting = [depth for _, depth in GROUPS]

    def send(way, hops, kib):
        nonlocal clock
        clock += ISSUE
        if abs(hops) == 2 and way == "y":
            ways, load = (("y", 1), ("y", -1)), 1.0
        else:
            ways, load = ((way, 1 if hops > 0 else -1),), abs(hops)
        begin = max([clock] + [free.get(w, 0.0) for w in ways])
        end = begin + load * 2 * kib * LINK
        for w in ways:
            free[w] = end
        return end + FIXED + HOP * abs(hops)

    trees = []
    for c, (row, rows, share, kind) in enumerate(chunks):
        edges = plane_tree(kind, c & 1)
        kids = {}
        for node, parent in edges:
            kids.setdefault(parent, []).append(node)
        trees.append((kids, len(edges)))
        pending.append((0.25 * c, c, ("node", c, (0, 0))))
    left = [n for _, n in trees]
    latest = [0.0] * len(chunks)
    order = []
    while pending:
        early = [e for e in pending if e[0] <= clock]
        pick = (
            min(early, key=lambda e: (e[2][0] == "compute", e[1], e[0]))
            if early
            else min(pending)
        )
        pending.remove(pick)
        clock = max(clock, pick[0]) + 0.03
        event = pick[2]
        what, c = event[0], event[1]
        if what == "compute":
            order.append(event)
            clock += PRODUCT * GROUPS[c][1] / 128 + 0.4
            continue
        row, rows, share, kind = chunks[c]
        each = rows // share
        kib = each / 2
        if what == "node":
            kids, _ = trees[c]
            nodes = kids[event[2]]
            order.append(("node", c, event[2], tuple(nodes)))
            for kid in nodes:
                dy, dz = hop_counts(kid, event[2])
                t = send("y", dy, kib) if dy else send("z", dz, kib)
                latest[c] = max(latest[c], t)
                left[c] -= 1
                if kid in kids:
                    pending.append((t, c, ("node", c, kid)))
            if left[c] == 0:
                pending.append((latest[c], c, ("select", c)))
        elif what == "select":
            order.append(event)
            clock += 0.1 + 0.004 * each
            if share == 4:
                t1, t2 = send("x", 1, 5 * kib), send("x", -1, 5 * kib)
                t3, t4 = send("x", 1, 5 * kib), send("x", -1, 5 * kib)
                arrived[c] = max(t3, t4)
                pending.append((max(t1, t2), c, ("forward", c)))
            elif share == 2:
                ready = max(send("x", 1, 5 * kib), send("x", -1, 5 * kib))
                pending.append((ready, c, ("arrive", c)))
            else:
                pending.append((clock, c, ("arrive", c)))
        elif what == "forward":
            order.append(event)
            ready = max(send("x", 1, 5 * kib), send("x", -1, 5 * kib), arrived[c])
            pending.append((ready, c, ("arrive", c)))
        else:
            order.append(event)
            for g, (first, depth) in enumerate(GROUPS):
                if first <= row < first + depth:
                    waiting[g] -= rows
                    if waiting[g] == 0:
                        pending.append((clock, g, ("compute", g)))
    return order, clock


def kernel(
    chunks, ints_hbm, orb_hbm, lists_hbm, counts_hbm, out_ref,
    ints, orb, acc, half, part, theirs, mine, coded, steps, other, *refs,
):
    count = len(chunks)
    tables, land = refs[:count], refs[count]
    (
        lists, counts, list_sem, int_sem, orb_sem, root_recv, leaf_recv, plane_send, x_recv, x_send,
        core_send, core_recv, sum_send, sum_recv, step_send, step_recv, last_send, last_recv,
    ) = refs[count + 1 :]
    slots = ints.shape[1]
    picks = slots - 1
    x = lax.axis_index("aux")
    plane = lax.axis_index("blk")
    core = lax.axis_index("occ")
    y, z = lax.rem(plane, NY), plane // NY

    def device(dx=0, dy=0, dz=0, dc=0):
        return (
            lax.rem(x + (dx + NX), NX),
            lax.rem(z + (dz + NZ), NZ) * NY + lax.rem(y + (dy + NY), NY),
            lax.rem(core + dc, 2),
        )

    def source(dy, dz):
        return lax.rem(z + (NZ - dz), NZ) * NY + lax.rem(y + (NY - dy), NY)

    int_copies = [
        pltpu.make_async_copy(ints_hbm.at[:, 0, 0], ints.at[:, 0], int_sem.at[0])
    ]
    for c, (row, rows) in enumerate(GROUPS):
        int_copies.append(
            pltpu.make_async_copy(
                ints_hbm.at[:, 0, pl.ds(1, slots - 1), :, pl.ds(row, rows)],
                ints.at[:, pl.ds(1, slots - 1), :, pl.ds(row, rows)],
                int_sem.at[c + 1],
            )
        )
    orb_copy = pltpu.make_async_copy(orb_hbm, orb, orb_sem)
    list_copies = (
        pltpu.make_async_copy(lists_hbm, lists, list_sem.at[0]),
        pltpu.make_async_copy(counts_hbm, counts, list_sem.at[1]),
    )
    orb_copy.start()
    for copy in list_copies:
        copy.start()
    int_copies[0].start()

    partners = {(1, 0, 0, 0), (3, 0, 0, 0), (2, 0, 0, 0), (0, 0, 0, 1)}
    for c, (_, _, _, kind) in enumerate(chunks):
        for node, parent in plane_tree(kind, c & 1):
            dy, dz = (node[0] - parent[0]) % NY, (node[1] - parent[1]) % NZ
            partners.add((0, dy, dz, 0))
            partners.add((0, -dy % NY, -dz % NZ, 0))
    barrier = pltpu.get_barrier_semaphore()
    for dx, dy, dz, dc in sorted(partners):
        pl.semaphore_signal(
            barrier, inc=1, device_id=device(dx, dy, dz, dc), device_id_type=MESH
        )
    orb_copy.wait()
    for copy in list_copies:
        copy.wait()
    pl.semaphore_wait(barrier, len(partners))

    def remote(src, dst, send, recv, target):
        return pltpu.make_async_remote_copy(
            src_ref=src, dst_ref=dst, send_sem=send, recv_sem=recv,
            device_id=target, device_id_type=MESH,
        )

    inner, leaves = {}, {}
    for c, (_, _, _, kind) in enumerate(chunks):
        edges = plane_tree(kind, c & 1)
        parents = {parent for _, parent in edges}
        nodes = [node for node, _ in edges if node in parents]
        inner[c] = {node: i for i, node in enumerate(nodes)}
        leaves[c] = len(edges) - len(nodes)

    def share_of(c):
        row, rows, share, _ = chunks[c]
        each = rows // share
        return row, each, (x if share == 4 else lax.rem(x, share))

    def do_node(c, node, kids):
        row, each, part_index = share_of(c)
        table = tables[c]
        block = source(*node)
        if node == (0, 0):
            first = pl.multiple_of(row + part_index * each, 16)
            src = orb.at[pl.ds(first, each)]
        else:
            src = table.at[block]
            remote(
                src, src, plane_send.at[c], root_recv.at[c, inner[c][node]], device(1)
            ).wait_recv()
        for kid in kids:
            recv = (
                root_recv.at[c, inner[c][kid]] if kid in inner[c] else leaf_recv.at[c]
            )
            remote(
                src, table.at[block], plane_send.at[c], recv,
                device(0, kid[0] - node[0], kid[1] - node[1]),
            ).start()
        if node == (0, 0):
            table[block] = orb[pl.ds(first, each)]

    def own_rows(c, part_index):
        row, each, _ = share_of(c)
        return pl.ds(pl.multiple_of(row + part_index * each, 16), each)

    def half_slots(c, part_index, which):
        return land.at[
            pl.ds(which * (picks // 2), picks // 2), own_rows(c, part_index)
        ]

    def x_copy(c, part_index, which, recv, dx):
        ref = half_slots(c, part_index, which)
        return remote(ref, ref, x_send.at[c], x_recv.at[c, recv], device(dx))

    def do_select(c):
        _, _, part_index = share_of(c)
        share = chunks[c][2]
        table, here = tables[c], own_rows(c, part_index)
        group = table.at[pl.ds(0, leaves[c])]
        remote(group, group, plane_send.at[c], leaf_recv.at[c], device(1)).wait_recv()
        live = counts[0]
        for s in range(picks):
            picked = table[lists[0, s + 1]]
            land[s, here] = jnp.where(s + 1 < live, picked, jnp.zeros_like(picked))
        if share == 4:
            x_copy(c, part_index, 0, 0, 1).start()
            x_copy(c, part_index, 1, 1, -1).start()
            x_copy(c, part_index, 1, 2, 1).start()
            x_copy(c, part_index, 0, 3, -1).start()
        elif share == 2:
            x_copy(c, part_index, 0, 0, 1).start()
            x_copy(c, part_index, 1, 1, -1).start()

    left, right, far = (lax.rem(x + k, NX) for k in (3, 1, 2))

    def do_forward(c):
        x_copy(c, left, 0, 0, 1).wait_recv()
        x_copy(c, left, 0, 4, 1).start()
        x_copy(c, right, 1, 1, -1).wait_recv()
        x_copy(c, right, 1, 5, -1).start()

    def do_arrive(c):
        share = chunks[c][2]
        if share == 4:
            x_copy(c, left, 1, 2, 1).wait_recv()
            x_copy(c, right, 0, 3, 1).wait_recv()
            x_copy(c, far, 0, 4, 1).wait_recv()
            x_copy(c, far, 1, 5, 1).wait_recv()
        elif share == 2:
            theirs_index = lax.rem(x + 1, 2)
            x_copy(c, theirs_index, 0, 0, 1).wait_recv()
            x_copy(c, theirs_index, 1, 1, 1).wait_recv()

    def product(g, p):
        row, rows = GROUPS[g]
        lhs = jnp.concatenate(
            [ints[p, s + 1, :, row : row + rows] for s in range(picks)], axis=1
        )
        rhs = land[:, row : row + rows].reshape(picks * rows, orb.shape[1])
        return acc[p] + jnp.dot(lhs, rhs, preferred_element_type=F32)

    order, _ = schedule(chunks)
    started, roots = False, 0
    for event in order:
        what, c = event[0], event[1]
        if what == "node":
            do_node(c, event[2], event[3])
        elif what == "select":
            do_select(c)
        elif what == "forward":
            do_forward(c)
        elif what == "arrive":
            do_arrive(c)
        else:
            int_copies[c + 1].wait()
            if event is not order[-1]:
                for p in range(4):
                    acc[p] = product(c, p)
        roots += what == "node" and event[2] == (0, 0)
        if not started and roots == count:
            started = True
            for copy in int_copies[1:]:
                copy.start()
            int_copies[0].wait()
            for p in range(4):
                acc[p] = jnp.dot(ints[p, 0], orb[...], preferred_element_type=F32)

    width = orb.shape[1]
    final = order[-1][1]
    for p in range(4):
        half[:, p * width : (p + 1) * width] = product(final, p).astype(BF16)

    basis = half.shape[0]
    kept = basis // NX
    sub = kept // 2
    scale = 1.0 / (2 * width)
    block = lax.dot_general(
        half[...], half[...], (((1,), (1,)), ((), ())), preferred_element_type=F32
    )
    part[...] = (block * scale).reshape(NX, 2, sub, basis)
    order = (2, 1, 3, 0)
    targets = [lax.rem(x + dx, NX) for dx in range(NX)]

    def core_copy(dx):
        return remote(
            part.at[targets[dx], 1 - core], theirs.at[dx], core_send.at[dx], core_recv.at[dx],
            device(dc=1),
        )

    def sum_copies(dx):
        return (
            remote(
                steps.at[dx, 0], steps.at[dx, 1], step_send.at[dx], step_recv.at[dx],
                device(dx),
            ),
            remote(
                coded.at[dx, 0], coded.at[dx, 1], sum_send.at[dx], sum_recv.at[dx],
                device(dx),
            ),
        )

    def encode(dx, value):
        parts = []
        for g in range(sub // 8):
            rows = value[8 * g : 8 * g + 8]
            top = jnp.max(jnp.abs(rows), axis=(0, 1), keepdims=True)
            step = jnp.maximum(top, 1e-33) * (1.0 / 32000.0)
            steps[dx, 0, g : g + 1] = jnp.broadcast_to(step, (1, 128))
            parts.append(jnp.round(rows * (1.0 / step)).astype(jnp.int32))
        coded[dx, 0] = jnp.concatenate(parts, axis=0).astype(jnp.int16)

    def decode(dx):
        whole = coded[dx, 1].astype(jnp.int32).astype(F32)
        size = steps[dx, 1]
        return jnp.concatenate(
            [
                whole[8 * g : 8 * g + 8] * size[g : g + 1, 0:1]
                for g in range(sub // 8)
            ],
            axis=0,
        )

    for dx in order:
        core_copy(dx).start()
    for dx in order:
        core_copy(dx).wait_recv()
        chip_sum = part[targets[dx], core] + theirs[dx]
        if dx:
            encode(dx, chip_sum)
            for copy in sum_copies(dx):
                copy.start()
    total = chip_sum
    for dx in (1, 3, 2):
        for copy in sum_copies(dx):
            copy.wait_recv()
        total = total + decode(dx)
    mine[...] = total
    last = remote(mine, other, last_send, last_recv, device(dc=1))
    last.start()
    out_ref[pl.ds(pl.multiple_of(core * sub, sub), sub)] = total
    last.wait_recv()
    out_ref[pl.ds(pl.multiple_of((1 - core) * sub, sub), sub)] = other[...]

    last.wait_send()
    for dx in order:
        core_copy(dx).wait_send()
        if dx:
            for copy in sum_copies(dx):
                copy.wait_send()
    for c, (_, _, share, kind) in enumerate(chunks):
        sent = tables[c].at[pl.ds(0, len(plane_tree(kind, c & 1)))]
        remote(sent, sent, plane_send.at[c], leaf_recv.at[c], device(1)).wait_send()
        if share == 4:
            sent = land.at[:, pl.ds(0, 3 * share_of(c)[1])]
        elif share == 2:
            sent = land.at[:, pl.ds(0, share_of(c)[1])]
        if share > 1:
            remote(sent, sent, x_send.at[c], leaf_recv.at[c], device(1)).wait_send()


def per_device(integrals, orbitals, pair_lists, pair_counts):
    aux, _, slots, basis, _ = integrals.shape
    width = orbitals.shape[1]
    picks = slots - 1
    kept = basis // NX
    count = len(CHUNKS)
    blocks = NY * NZ
    dma = pltpu.SemaphoreType.DMA
    scratch = [
        pltpu.VMEM((aux, slots, basis, basis), BF16),
        pltpu.VMEM((basis, width), BF16),
        pltpu.VMEM((aux, basis, width), F32),
        pltpu.VMEM((basis, aux * width), BF16),
        pltpu.VMEM((NX, 2, kept // 2, basis), F32),
        pltpu.VMEM((NX, kept // 2, basis), F32),
        pltpu.VMEM((kept // 2, basis), F32),
        pltpu.VMEM((NX, 2, kept // 2, basis), jnp.int16),
        pltpu.VMEM((NX, 2, kept // 16, 128), F32),
        pltpu.VMEM((kept // 2, basis), F32),
    ]
    scratch += [pltpu.VMEM((blocks, n // g, width), BF16) for _, n, g, _ in CHUNKS]
    scratch += [pltpu.VMEM((picks, basis, width), BF16)]
    scratch += [
        pltpu.SMEM((1, slots), jnp.int32), pltpu.SMEM((1,), jnp.int32), dma((2,)),
        dma((len(GROUPS) + 1,)), dma, dma((count, 32)), dma((count,)), dma((count,)),
        dma((count, 6)), dma((count,)),
        dma((NX,)), dma((NX,)), dma((NX,)), dma((NX,)), dma((NX,)), dma((NX,)), dma, dma,
    ]
    result = pl.pallas_call(
        functools.partial(kernel, CHUNKS),
        out_shape=jax.ShapeDtypeStruct((kept, basis), F32),
        in_specs=[
            pl.BlockSpec(memory_space=pl.ANY),
            pl.BlockSpec(memory_space=pl.ANY),
            pl.BlockSpec(memory_space=pl.ANY),
            pl.BlockSpec(memory_space=pl.ANY),
        ],
        out_specs=pl.BlockSpec(memory_space=pltpu.VMEM),
        scratch_shapes=scratch,
        name="exchange_blocks",
        compiler_params=pltpu.CompilerParams(
            collective_id=0, has_side_effects=True, vmem_limit_bytes=214 * 2**18
        ),
    )(integrals, orbitals, pair_lists, pair_counts)
    return result[None]


def solution(mesh):
    placed = (P("aux", "blk", None, None, None), P("blk", "occ"), P("blk", None), P("blk"))
    return jax.shard_map(
        per_device, mesh=mesh, in_specs=placed, out_specs=P("blk", "aux", None), check_vma=False
    )
```

```python
import functools

import jax
import jax.numpy as jnp
from jax import lax
from jax.experimental import pallas as pl
from jax.experimental.pallas import tpu as pltpu
from jax.sharding import PartitionSpec as P

MESH = pl.DeviceIdType.MESH
NX, NY, NZ = 4, 4, 8
BF16, F32 = jnp.bfloat16, jnp.float32

CHUNKS = (
    (0, 128, 4, "zy quick direct"),
    (128, 128, 4, "yz fwd fwd"),
    (256, 128, 4, "yz fwd direct"),
    (384, 128, 1, "zy fwd fwd"),
)
GROUPS = ((0, 128), (128, 128), (256, 128), (384, 128))


def z_tree(kind, flip):
    if kind == "direct":
        return [(k, 0) for k in (1, -1, 2, -2, 3, -3, 4)]
    if kind == "quick":
        edges = [(1, 0), (-1, 0), (2, 0), (-2, 0), (3, 2), (-3, -2), (4, 2)]
    else:
        edges = [(1, 0), (-1, 0), (2, 1), (-2, -1), (3, 2), (-3, -2), (4, 3)]
    if flip:
        edges[-1] = (-4, -edges[-1][1])
    return edges


def y_tree(kind, flip):
    if kind == "direct":
        return [(1, 0), (-1, 0), (2, 0)]
    return [(1, 0), (-1, 0), (-2, -1) if flip else (2, 1)]


def plane_tree(kind, flip):
    first, z_kind, y_kind = kind.split()
    edges = []
    if first == "zy":
        for dz, parent in [(0, None)] + z_tree(z_kind, flip):
            if parent is not None:
                edges.append(((0, dz), (0, parent)))
        for dz, _ in [(0, None)] + z_tree(z_kind, flip):
            for dy, parent in y_tree(y_kind, flip ^ (dz & 1)):
                edges.append(((dy, dz), (parent, dz)))
    else:
        for dy, parent in y_tree(y_kind, flip):
            edges.append(((dy, 0), (parent, 0)))
        for dy, _ in [(0, None)] + y_tree(y_kind, flip):
            for dz, parent in z_tree(z_kind, flip ^ (dy & 1)):
                edges.append(((dy, dz), (dy, parent)))
    return edges


def hop_counts(node, parent):
    return node[0] - parent[0], node[1] - parent[1]


LINK = 0.01
ISSUE, FIXED, HOP = 0.04, 1.8, 0.65
PRODUCT = 1.2


def schedule(chunks):
    free = {}
    clock = 0.0
    pending = []
    arrived = {}
    waiting = [depth for _, depth in GROUPS]

    def send(way, hops, kib):
        nonlocal clock
        clock += ISSUE
        if abs(hops) == 2 and way == "y":
            ways, load = (("y", 1), ("y", -1)), 1.0
        else:
            ways, load = ((way, 1 if hops > 0 else -1),), abs(hops)
        begin = max([clock] + [free.get(w, 0.0) for w in ways])
        end = begin + load * 2 * kib * LINK
        for w in ways:
            free[w] = end
        return end + FIXED + HOP * abs(hops)

    trees = []
    for c, (row, rows, share, kind) in enumerate(chunks):
        edges = plane_tree(kind, c & 1)
        kids = {}
        for node, parent in edges:
            kids.setdefault(parent, []).append(node)
        trees.append((kids, len(edges)))
        pending.append((0.25 * c, c, ("node", c, (0, 0))))
    left = [n for _, n in trees]
    latest = [0.0] * len(chunks)
    order = []
    while pending:
        early = [e for e in pending if e[0] <= clock]
        pick = (
            min(early, key=lambda e: (e[2][0] == "compute", e[1], e[0]))
            if early
            else min(pending)
        )
        pending.remove(pick)
        clock = max(clock, pick[0]) + 0.03
        event = pick[2]
        what, c = event[0], event[1]
        if what == "compute":
            order.append(event)
            clock += PRODUCT * GROUPS[c][1] / 128 + 0.4
            continue
        row, rows, share, kind = chunks[c]
        each = rows // share
        kib = each / 2
        if what == "node":
            kids, _ = trees[c]
            nodes = kids[event[2]]
            order.append(("node", c, event[2], tuple(nodes)))
            for kid in nodes:
                dy, dz = hop_counts(kid, event[2])
                t = send("y", dy, kib) if dy else send("z", dz, kib)
                latest[c] = max(latest[c], t)
                left[c] -= 1
                if kid in kids:
                    pending.append((t, c, ("node", c, kid)))
            if left[c] == 0:
                pending.append((latest[c], c, ("select", c)))
        elif what == "select":
            order.append(event)
            clock += 0.1 + 0.004 * each
            if share == 4:
                t1, t2 = send("x", 1, 5 * kib), send("x", -1, 5 * kib)
                t3, t4 = send("x", 1, 5 * kib), send("x", -1, 5 * kib)
                arrived[c] = max(t3, t4)
                pending.append((max(t1, t2), c, ("forward", c)))
            elif share == 2:
                ready = max(send("x", 1, 5 * kib), send("x", -1, 5 * kib))
                pending.append((ready, c, ("arrive", c)))
            else:
                pending.append((clock, c, ("arrive", c)))
        elif what == "forward":
            order.append(event)
            ready = max(send("x", 1, 5 * kib), send("x", -1, 5 * kib), arrived[c])
            pending.append((ready, c, ("arrive", c)))
        else:
            order.append(event)
            for g, (first, depth) in enumerate(GROUPS):
                if first <= row < first + depth:
                    waiting[g] -= rows
                    if waiting[g] == 0:
                        pending.append((clock, g, ("compute", g)))
    return order, clock


def kernel(
    chunks, ints_hbm, orb_hbm, lists_hbm, counts_hbm, out_ref,
    ints, orb, acc, half, part, theirs, mine, coded, steps, other, *refs,
):
    count = len(chunks)
    tables, land = refs[:count], refs[count]
    (
        lists, counts, list_sem, int_sem, orb_sem, root_recv, leaf_recv, plane_send, x_recv, x_send,
        core_send, core_recv, sum_send, sum_recv, step_send, step_recv, last_send, last_recv,
    ) = refs[count + 1 :]
    slots = ints.shape[1]
    picks = slots - 1
    x = lax.axis_index("aux")
    plane = lax.axis_index("blk")
    core = lax.axis_index("occ")
    y, z = lax.rem(plane, NY), plane // NY

    def device(dx=0, dy=0, dz=0, dc=0):
        return (
            lax.rem(x + (dx + NX), NX),
            lax.rem(z + (dz + NZ), NZ) * NY + lax.rem(y + (dy + NY), NY),
            lax.rem(core + dc, 2),
        )

    def source(dy, dz):
        return lax.rem(z + (NZ - dz), NZ) * NY + lax.rem(y + (NY - dy), NY)

    int_copies = [
        pltpu.make_async_copy(ints_hbm.at[:, 0, 0], ints.at[:, 0], int_sem.at[0])
    ]
    for c, (row, rows) in enumerate(GROUPS):
        int_copies.append(
            pltpu.make_async_copy(
                ints_hbm.at[:, 0, pl.ds(1, slots - 1), :, pl.ds(row, rows)],
                ints.at[:, pl.ds(1, slots - 1), :, pl.ds(row, rows)],
                int_sem.at[c + 1],
            )
        )
    orb_copy = pltpu.make_async_copy(orb_hbm, orb, orb_sem)
    list_copies = (
        pltpu.make_async_copy(lists_hbm, lists, list_sem.at[0]),
        pltpu.make_async_copy(counts_hbm, counts, list_sem.at[1]),
    )
    orb_copy.start()
    for copy in list_copies:
        copy.start()
    int_copies[0].start()

    partners = {(1, 0, 0, 0), (3, 0, 0, 0), (2, 0, 0, 0), (0, 0, 0, 1)}
    for c, (_, _, _, kind) in enumerate(chunks):
        for node, parent in plane_tree(kind, c & 1):
            dy, dz = (node[0] - parent[0]) % NY, (node[1] - parent[1]) % NZ
            partners.add((0, dy, dz, 0))
            partners.add((0, -dy % NY, -dz % NZ, 0))
    barrier = pltpu.get_barrier_semaphore()
    for dx, dy, dz, dc in sorted(partners):
        pl.semaphore_signal(
            barrier, inc=1, device_id=device(dx, dy, dz, dc), device_id_type=MESH
        )
    orb_copy.wait()
    for copy in list_copies:
        copy.wait()
    pl.semaphore_wait(barrier, len(partners))

    def remote(src, dst, send, recv, target):
        return pltpu.make_async_remote_copy(
            src_ref=src, dst_ref=dst, send_sem=send, recv_sem=recv,
            device_id=target, device_id_type=MESH,
        )

    inner, leaves = {}, {}
    for c, (_, _, _, kind) in enumerate(chunks):
        edges = plane_tree(kind, c & 1)
        parents = {parent for _, parent in edges}
        nodes = [node for node, _ in edges if node in parents]
        inner[c] = {node: i for i, node in enumerate(nodes)}
        leaves[c] = len(edges) - len(nodes)

    def share_of(c):
        row, rows, share, _ = chunks[c]
        each = rows // share
        return row, each, (x if share == 4 else lax.rem(x, share))

    def do_node(c, node, kids):
        row, each, part_index = share_of(c)
        table = tables[c]
        block = source(*node)
        if node == (0, 0):
            first = pl.multiple_of(row + part_index * each, 16)
            src = orb.at[pl.ds(first, each)]
        else:
            src = table.at[block]
            remote(
                src, src, plane_send.at[c], root_recv.at[c, inner[c][node]], device(1)
            ).wait_recv()
        for kid in kids:
            recv = (
                root_recv.at[c, inner[c][kid]] if kid in inner[c] else leaf_recv.at[c]
            )
            remote(
                src, table.at[block], plane_send.at[c], recv,
                device(0, kid[0] - node[0], kid[1] - node[1]),
            ).start()
        if node == (0, 0):
            table[block] = orb[pl.ds(first, each)]

    def own_rows(c, part_index):
        row, each, _ = share_of(c)
        return pl.ds(pl.multiple_of(row + part_index * each, 16), each)

    def half_slots(c, part_index, which):
        return land.at[
            pl.ds(which * (picks // 2), picks // 2), own_rows(c, part_index)
        ]

    def x_copy(c, part_index, which, recv, dx):
        ref = half_slots(c, part_index, which)
        return remote(ref, ref, x_send.at[c], x_recv.at[c, recv], device(dx))

    def do_select(c):
        _, _, part_index = share_of(c)
        share = chunks[c][2]
        table, here = tables[c], own_rows(c, part_index)
        group = table.at[pl.ds(0, leaves[c])]
        remote(group, group, plane_send.at[c], leaf_recv.at[c], device(1)).wait_recv()
        live = counts[0]
        for s in range(picks):
            picked = table[lists[0, s + 1]]
            land[s, here] = jnp.where(s + 1 < live, picked, jnp.zeros_like(picked))
        if share == 4:
            x_copy(c, part_index, 0, 0, 1).start()
            x_copy(c, part_index, 1, 1, -1).start()
            x_copy(c, part_index, 1, 2, 1).start()
            x_copy(c, part_index, 0, 3, -1).start()
        elif share == 2:
            x_copy(c, part_index, 0, 0, 1).start()
            x_copy(c, part_index, 1, 1, -1).start()

    left, right, far = (lax.rem(x + k, NX) for k in (3, 1, 2))

    def do_forward(c):
        x_copy(c, left, 0, 0, 1).wait_recv()
        x_copy(c, left, 0, 4, 1).start()
        x_copy(c, right, 1, 1, -1).wait_recv()
        x_copy(c, right, 1, 5, -1).start()

    def do_arrive(c):
        share = chunks[c][2]
        if share == 4:
            x_copy(c, left, 1, 2, 1).wait_recv()
            x_copy(c, right, 0, 3, 1).wait_recv()
            x_copy(c, far, 0, 4, 1).wait_recv()
            x_copy(c, far, 1, 5, 1).wait_recv()
        elif share == 2:
            theirs_index = lax.rem(x + 1, 2)
            x_copy(c, theirs_index, 0, 0, 1).wait_recv()
            x_copy(c, theirs_index, 1, 1, 1).wait_recv()

    def product(g, p):
        row, rows = GROUPS[g]
        lhs = jnp.concatenate(
            [ints[p, s + 1, :, row : row + rows] for s in range(picks)], axis=1
        )
        rhs = land[:, row : row + rows].reshape(picks * rows, orb.shape[1])
        return acc[p] + jnp.dot(lhs, rhs, preferred_element_type=F32)

    order, _ = schedule(chunks)
    started, roots = False, 0
    for event in order:
        what, c = event[0], event[1]
        if what == "node":
            do_node(c, event[2], event[3])
        elif what == "select":
            do_select(c)
        elif what == "forward":
            do_forward(c)
        elif what == "arrive":
            do_arrive(c)
        else:
            int_copies[c + 1].wait()
            if event is not order[-1]:
                for p in range(4):
                    acc[p] = product(c, p)
        roots += what == "node" and event[2] == (0, 0)
        if not started and roots == count:
            started = True
            for copy in int_copies[1:]:
                copy.start()
            int_copies[0].wait()
            for p in range(4):
                acc[p] = jnp.dot(ints[p, 0], orb[...], preferred_element_type=F32)

    width = orb.shape[1]
    final = order[-1][1]
    for p in range(4):
        half[:, p * width : (p + 1) * width] = product(final, p).astype(BF16)

    basis = half.shape[0]
    kept = basis // NX
    sub = kept // 2
    scale = 1.0 / (2 * width)
    block = lax.dot_general(
        half[...], half[...], (((1,), (1,)), ((), ())), preferred_element_type=F32
    )
    part[...] = (block * scale).reshape(NX, 2, sub, basis)
    order = (2, 1, 3, 0)
    targets = [lax.rem(x + dx, NX) for dx in range(NX)]

    def core_copy(dx):
        return remote(
            part.at[targets[dx], 1 - core], theirs.at[dx], core_send.at[dx], core_recv.at[dx],
            device(dc=1),
        )

    def sum_copies(dx):
        return (
            remote(
                steps.at[dx, 0], steps.at[dx, 1], step_send.at[dx], step_recv.at[dx],
                device(dx),
            ),
            remote(
                coded.at[dx, 0], coded.at[dx, 1], sum_send.at[dx], sum_recv.at[dx],
                device(dx),
            ),
        )

    def encode(dx, value):
        parts = []
        for g in range(sub // 8):
            rows = value[8 * g : 8 * g + 8]
            top = jnp.max(jnp.abs(rows), axis=(0, 1), keepdims=True)
            step = jnp.maximum(top, 1e-33) * (1.0 / 32000.0)
            steps[dx, 0, g : g + 1] = jnp.broadcast_to(step, (1, 128))
            parts.append(jnp.round(rows * (1.0 / step)).astype(jnp.int32))
        coded[dx, 0] = jnp.concatenate(parts, axis=0).astype(jnp.int16)

    def decode(dx, first, rows):
        whole = coded[dx, 1, first : first + rows].astype(jnp.int32).astype(F32)
        size = steps[dx, 1]
        return jnp.concatenate(
            [
                whole[8 * g : 8 * g + 8] * size[first // 8 + g : first // 8 + g + 1, 0:1]
                for g in range(rows // 8)
            ],
            axis=0,
        )

    for dx in order:
        core_copy(dx).start()
    for dx in order:
        core_copy(dx).wait_recv()
        chip_sum = part[targets[dx], core] + theirs[dx]
        if dx:
            encode(dx, chip_sum)
            for copy in sum_copies(dx):
                copy.start()
    for dx in (1, 3, 2):
        for copy in sum_copies(dx):
            copy.wait_recv()
    parts, rows = 2, sub // 2
    lasts = []
    for n in range(parts):
        first = n * rows
        total = chip_sum[first : first + rows]
        for dx in (1, 3, 2):
            total = total + decode(dx, first, rows)
        mine[first : first + rows] = total
        last = remote(
            mine.at[pl.ds(first, rows)], other.at[pl.ds(first, rows)],
            last_send.at[n], last_recv.at[n], device(dc=1),
        )
        last.start()
        lasts.append(last)
        out_ref[pl.ds(pl.multiple_of(core * sub + first, 8), rows)] = total
    for n, last in enumerate(lasts):
        first = n * rows
        last.wait_recv()
        out_ref[pl.ds(pl.multiple_of((1 - core) * sub + first, 8), rows)] = other[
            first : first + rows
        ]

    for last in lasts:
        last.wait_send()
    for dx in order:
        core_copy(dx).wait_send()
        if dx:
            for copy in sum_copies(dx):
                copy.wait_send()
    for c, (_, _, share, kind) in enumerate(chunks):
        sent = tables[c].at[pl.ds(0, len(plane_tree(kind, c & 1)))]
        remote(sent, sent, plane_send.at[c], leaf_recv.at[c], device(1)).wait_send()
        if share == 4:
            sent = land.at[:, pl.ds(0, 3 * share_of(c)[1])]
        elif share == 2:
            sent = land.at[:, pl.ds(0, share_of(c)[1])]
        if share > 1:
            remote(sent, sent, x_send.at[c], leaf_recv.at[c], device(1)).wait_send()


def per_device(integrals, orbitals, pair_lists, pair_counts):
    aux, _, slots, basis, _ = integrals.shape
    width = orbitals.shape[1]
    picks = slots - 1
    kept = basis // NX
    count = len(CHUNKS)
    blocks = NY * NZ
    dma = pltpu.SemaphoreType.DMA
    scratch = [
        pltpu.VMEM((aux, slots, basis, basis), BF16),
        pltpu.VMEM((basis, width), BF16),
        pltpu.VMEM((aux, basis, width), F32),
        pltpu.VMEM((basis, aux * width), BF16),
        pltpu.VMEM((NX, 2, kept // 2, basis), F32),
        pltpu.VMEM((NX, kept // 2, basis), F32),
        pltpu.VMEM((kept // 2, basis), F32),
        pltpu.VMEM((NX, 2, kept // 2, basis), jnp.int16),
        pltpu.VMEM((NX, 2, kept // 16, 128), F32),
        pltpu.VMEM((kept // 2, basis), F32),
    ]
    scratch += [pltpu.VMEM((blocks, n // g, width), BF16) for _, n, g, _ in CHUNKS]
    scratch += [pltpu.VMEM((picks, basis, width), BF16)]
    scratch += [
        pltpu.SMEM((1, slots), jnp.int32), pltpu.SMEM((1,), jnp.int32), dma((2,)),
        dma((len(GROUPS) + 1,)), dma, dma((count, 32)), dma((count,)), dma((count,)),
        dma((count, 6)), dma((count,)),
        dma((NX,)), dma((NX,)), dma((NX,)), dma((NX,)), dma((NX,)), dma((NX,)), dma((2,)), dma((2,)),
    ]
    result = pl.pallas_call(
        functools.partial(kernel, CHUNKS),
        out_shape=jax.ShapeDtypeStruct((kept, basis), F32),
        in_specs=[
            pl.BlockSpec(memory_space=pl.ANY),
            pl.BlockSpec(memory_space=pl.ANY),
            pl.BlockSpec(memory_space=pl.ANY),
            pl.BlockSpec(memory_space=pl.ANY),
        ],
        out_specs=pl.BlockSpec(memory_space=pltpu.VMEM),
        scratch_shapes=scratch,
        name="exchange_blocks",
        compiler_params=pltpu.CompilerParams(
            collective_id=0, has_side_effects=True, vmem_limit_bytes=214 * 2**18
        ),
    )(integrals, orbitals, pair_lists, pair_counts)
    return result[None]


def solution(mesh):
    placed = (P("aux", "blk", None, None, None), P("blk", "occ"), P("blk", None), P("blk"))
    return jax.shard_map(
        per_device, mesh=mesh, in_specs=placed, out_specs=P("blk", "aux", None), check_vma=False
    )
```
